32 devices in a mesh: groups: 2 (over x), expert: 4 (over y, core), dp: 4 (over z).
Axes of the slice: x: 2, y: 2, z: 4, core: 2. Of those that a mesh axis runs over, the one named last changes fastest.
Arguments:
- tokens: bfloat16 [6144, 2048], P(('groups', 'expert', 'dp')), parts along dimension 0, may hold values from -6 to 6
- expert_ids: int32 [6144, 2], P(('groups', 'expert', 'dp')), parts along dimension 0, may hold values from 0 to 3, all different within a row; in each aligned block of 192 rows (0 to 191, 192 to 383, ...) at most 128 rows name the same one
- gate_weights: float32 [6144, 2], P(('groups', 'expert', 'dp')), parts along dimension 0, may hold values from 0.1 to 1
- out_grad: bfloat16 [6144, 2048], P(('groups', 'expert', 'dp')), parts along dimension 0, may hold values from -1.5 to 1.5
- w_gate: bfloat16 [4, 2048, 768], P('expert'), may hold values from -0.125 to 0.125
- w_up: bfloat16 [4, 2048, 768], P('expert'), may hold values from -0.125 to 0.125
- w_down: bfloat16 [4, 768, 2048], P('expert'), may hold values from -0.21875 to 0.21875
Outputs:
- token_grads: bfloat16 [6144, 2048], P(('groups', 'expert', 'dp')), parts along dimension 0
- gate_grads: float32 [6144, 2], P(('groups', 'expert', 'dp')), parts along dimension 0
- grad_gate: bfloat16 [8, 2048, 768], P(('groups', 'expert'), 'dp'), parts along dimension 0
- grad_up: bfloat16 [8, 2048, 768], P(('groups', 'expert'), 'dp'), parts along dimension 0
- grad_down: bfloat16 [8, 768, 2048], P(('groups', 'expert'), None, 'dp'), parts along dimension 0
The draws below stay inside these ranges and needn't reach their ends.
There are 2 independent parts, one for each index of `groups`. The reference program is written for one: setup_inputs(seed, part) draws one part's arguments, and reference() takes and returns one part's arrays. A program takes and returns all parts, laid end to end along the dimension named above; an argument that names none is the same for every part. Nothing has to cross between parts.
Inputs may be any that keep to these rules, and one draw needn't show every extreme that they name: `expert_ids`: A token's 2 picks name different experts. Within the rows of one device no expert is named by more than 128 picks, and in every draw some device names some expert exactly 128 times.
All inputs are finite; a program needn't handle non-finite values.
Results may differ from the reference program's by a relative error of at most 0.009.
Values may be sent and summed in bfloat16 or wider, within the bound.
No kernel may reach another device: no remote copies, remote signals or barrier semaphores. Data moves between devices by JAX's collectives and lax.ppermute only.
A program may use at most 128 MiB of HBM per device.

```python
import math
import jax
import jax.numpy as jnp
import numpy as np
from jax import lax

D = 2048
FF = 768
TOK_DEV = 192
TOP = 2
EXPERTS = 4
CAP = 128
TOKENS = 3072
N_EXPERT = 4
N_DP = 4


def block_levels(own_key, shape, pieces, least, top_value):
    def one(dim, parts):
        steps = jax.random.uniform(jax.random.fold_in(jax.random.fold_in(own_key, 6), dim), (parts,), jnp.float32, least / len(pieces), top_value / len(pieces))
        return jnp.repeat(jnp.exp(steps), shape[dim] // parts).reshape((-1,) + (1,) * (len(shape) - dim - 1))

    gain = one(*pieces[0])
    for cut in pieces[1:]:
        gain = gain * one(*cut)
    return gain


def routed_block(key, own, number, rows, amount, top, most, lean):
    sequence = jax.random.permutation(key, amount)
    crowded, ordinary = shares(amount, rows * top, most, lean, True), shares(amount, rows * top, most, lean, False)
    places = jnp.arange(amount)

    def named(sizes, offset_by):
        used = int((sizes > 0).sum())
        fixed = max(1, used // 4)
        moved = fixed + (places - fixed + offset_by * (used - fixed)) % max(1, amount - fixed)
        return jnp.zeros((amount,), jnp.int32).at[sequence[jnp.where(places < fixed, places, moved)]].set(jnp.asarray(sizes, jnp.int32))

    sizes = jnp.where(number % 4 == 0, named(crowded, number // 4), named(ordinary, number - number // 4 - 1))
    mixed = jax.random.permutation(jax.random.fold_in(own, 3), amount)
    source_of, receiver = mixed[0:amount // 2 * 2:2], mixed[1:amount // 2 * 2:2]
    margin = jnp.minimum(sizes[source_of] - 1, most - sizes[receiver]) // 2
    margin = jnp.where((source_of == sequence[0]) | (receiver == sequence[0]) | (sizes[receiver] == 0), 0, jnp.maximum(margin, 0))
    moved = jax.random.randint(jax.random.fold_in(own, 4), (amount // 2,), 0, 1 << 20) % (margin + 1)
    sizes = sizes.at[source_of].add(-moved).at[receiver].add(moved)
    items = jnp.searchsorted(jnp.cumsum(sizes), jnp.arange(rows * top), side="right").astype(jnp.int32)
    listing = items.reshape(top, rows).T
    listing = listing[jax.random.permutation(jax.random.fold_in(own, 1), rows)]
    offset_by = jax.random.randint(jax.random.fold_in(own, 2), (rows, 1), 0, top)
    return jnp.take_along_axis(listing, (jnp.arange(top)[None, :] + offset_by) % top, axis=1)


def shares(number_of, total, reach, skew, full):
    loads = [(1 << 20) // math.isqrt(rank ** skew) + 1 for rank in range(1, number_of + 1)]
    largest = reach if full else min(reach, max(-(-total // number_of), total * loads[0] // sum(loads)))
    least = 1 if total - largest >= number_of - 1 else 0
    holding, spare = [largest] + [least] * (number_of - 1), total - largest - least * (number_of - 1)
    while spare > 0:
        free = [i for i in range(1, number_of) if holding[i] < largest] or [i for i in range(1, number_of) if holding[i] < reach]
        mass, left = sum([loads[i] for i in free]), spare
        for i in free:
            addition = min(reach - holding[i], max(1, left * loads[i] // mass), spare)
            holding[i] = holding[i] + addition
            spare = spare - addition
    return np.array(holding)


def gaussian(rng, dims, spread, bound, shards=(), kind=jnp.bfloat16):
    gain = block_levels(rng, dims, shards, -0.22, 0.18) if shards else 1.0
    entries = jax.random.normal(rng, dims, jnp.float32) * spread * gain
    return jnp.minimum(jnp.maximum(entries, -bound), bound).astype(kind)


def setup_inputs(seed: int = 0, part: int = 0) -> dict:
    key_of = jax.random.split(jax.random.key(seed), 8)
    part_splits = jax.random.split(jax.random.fold_in(key_of[7], part), 8)
    tokens = gaussian(part_splits[0], (TOKENS, D), 1.0, 6.0, ((0, 16),))
    expert_ids_keys = jax.random.split(jax.random.fold_in(part_splits[1], 1), TOKENS // TOK_DEV)
    expert_ids_turns = jax.random.permutation(jax.random.fold_in(part_splits[1], 3), TOKENS // TOK_DEV)
    expert_ids = jax.vmap(lambda own, number: routed_block(jax.random.fold_in(part_splits[1], 2), own, number, TOK_DEV, EXPERTS, TOP, CAP, 2))(expert_ids_keys, expert_ids_turns).reshape((TOKENS, TOP))
    gate_weights = jnp.clip(0.1 + 0.9 * jax.random.uniform(part_splits[2], (TOKENS, TOP), jnp.float32) ** block_levels(part_splits[2], (TOKENS, TOP), ((0, 16),), -0.2, 0.2), 0.1, 1.0)
    out_grad = gaussian(part_splits[3], (TOKENS, D), 0.25, 1.5, ((0, 16),))
    w_gate = gaussian(key_of[4], (EXPERTS, D, FF), D ** -0.5, 0.125, ((0, 4),))
    w_up = gaussian(key_of[5], (EXPERTS, D, FF), D ** -0.5, 0.125, ((0, 4),))
    w_down = gaussian(key_of[6], (EXPERTS, FF, D), FF ** -0.5, 0.21875, ((0, 4),))
    return dict(tokens=tokens, expert_ids=expert_ids, gate_weights=gate_weights, out_grad=out_grad, w_gate=w_gate, w_up=w_up, w_down=w_down)


def rows_pass(rows_x, rows_grad, gate_w, up_w, down_w):
    gate_pre = jnp.dot(rows_x, gate_w, preferred_element_type=jnp.float32)
    up_pre = jnp.dot(rows_x, up_w, preferred_element_type=jnp.float32)
    sigmoid = jax.nn.sigmoid(gate_pre)
    activated = gate_pre * sigmoid
    hidden = (activated * up_pre).astype(jnp.bfloat16)
    expert_out = jnp.dot(hidden, down_w, preferred_element_type=jnp.float32).astype(jnp.bfloat16)
    hidden_grad = jnp.dot(rows_grad, down_w.T, preferred_element_type=jnp.float32)
    gate_pre_grad = (hidden_grad * up_pre * (sigmoid * (1.0 + gate_pre * (1.0 - sigmoid)))).astype(jnp.bfloat16)
    up_pre_grad = (hidden_grad * activated).astype(jnp.bfloat16)
    input_grad = (jnp.dot(gate_pre_grad, gate_w.T, preferred_element_type=jnp.float32)
                  + jnp.dot(up_pre_grad, up_w.T, preferred_element_type=jnp.float32)).astype(jnp.bfloat16)
    grad_g = jnp.dot(rows_x.T, gate_pre_grad, preferred_element_type=jnp.float32)
    grad_u = jnp.dot(rows_x.T, up_pre_grad, preferred_element_type=jnp.float32)
    grad_d = jnp.dot(hidden.T, rows_grad, preferred_element_type=jnp.float32)
    return expert_out, input_grad, grad_g, grad_u, grad_d


def reference(tokens, expert_ids, gate_weights, out_grad, w_gate, w_up, w_down):
    slot_total = N_EXPERT * CAP
    picks_total = TOKENS * TOP
    token_index = jnp.arange(TOKENS, dtype=jnp.int32).reshape(N_EXPERT, N_DP, TOK_DEV)
    ids_grouped = expert_ids.reshape(N_EXPERT, N_DP, TOK_DEV * TOP)
    flat_gate = gate_weights.reshape(-1)
    pick_slot = jnp.tile(jnp.arange(TOP, dtype=jnp.int32), N_EXPERT * TOK_DEV)

    def one_pair(carry, pair):
        tok_acc, gate_acc = carry
        expert = (pair // N_DP).astype(jnp.int32)
        replica = (pair % N_DP).astype(jnp.int32)
        group_ids = lax.dynamic_index_in_dim(ids_grouped, replica, 1, keepdims=False).reshape(-1)
        group_tok = lax.dynamic_index_in_dim(token_index, replica, 1, keepdims=False).reshape(-1)
        group_pick = jnp.repeat(group_tok, TOP) * TOP + pick_slot
        row_order = jnp.argsort((group_ids != expert).astype(jnp.int32), stable=True)[:slot_total]
        live_count = jnp.sum((group_ids == expert).astype(jnp.int32))
        live_rows = jnp.arange(slot_total, dtype=jnp.int32) < live_count
        chosen = group_pick[row_order]
        chosen_tok = chosen // TOP
        rows_x = jnp.where(live_rows[:, None], tokens[chosen_tok], jnp.zeros((), jnp.bfloat16))
        scaled = (flat_gate[chosen][:, None] * out_grad[chosen_tok].astype(jnp.float32)).astype(jnp.bfloat16)
        rows_grad = jnp.where(live_rows[:, None], scaled, jnp.zeros((), jnp.bfloat16))
        gate_w = lax.dynamic_index_in_dim(w_gate, expert, 0, keepdims=False)
        up_w = lax.dynamic_index_in_dim(w_up, expert, 0, keepdims=False)
        down_w = lax.dynamic_index_in_dim(w_down, expert, 0, keepdims=False)
        expert_out, input_grad, grad_g, grad_u, grad_d = rows_pass(rows_x, rows_grad, gate_w, up_w, down_w)
        pick_gate_grad = jnp.sum(out_grad[chosen_tok].astype(jnp.float32) * expert_out.astype(jnp.float32), axis=1)
        pick_target = jnp.where(live_rows, chosen, picks_total)
        tok_target = jnp.where(live_rows, chosen_tok, TOKENS)
        gate_acc = gate_acc.at[pick_target].add(pick_gate_grad, mode="drop")
        tok_acc = tok_acc.at[tok_target].add(input_grad.astype(jnp.float32), mode="drop")
        partial_value = (grad_g.astype(jnp.bfloat16), grad_u.astype(jnp.bfloat16), grad_d.astype(jnp.bfloat16))
        return (tok_acc, gate_acc), partial_value

    start = (jnp.zeros((TOKENS, D), jnp.float32), jnp.zeros((picks_total,), jnp.float32))
    (tok_acc, gate_acc), partial_value = lax.scan(one_pair, start, jnp.arange(N_EXPERT * N_DP, dtype=jnp.int32))
    grad_gate = jnp.sum(partial_value[0].reshape(EXPERTS, N_DP, D, FF).astype(jnp.float32), axis=1).astype(jnp.bfloat16)
    grad_up = jnp.sum(partial_value[1].reshape(EXPERTS, N_DP, D, FF).astype(jnp.float32), axis=1).astype(jnp.bfloat16)
    grad_down = jnp.sum(partial_value[2].reshape(EXPERTS, N_DP, FF, D).astype(jnp.float32), axis=1).astype(jnp.bfloat16)
    return (tok_acc.astype(jnp.bfloat16), gate_acc.reshape(TOKENS, TOP), grad_gate, grad_up, grad_down)
```

```python
import jax
import jax.numpy as jnp
from jax import lax
from jax.sharding import PartitionSpec as P

BF = jnp.bfloat16
F32 = jnp.float32


def dot(a, b, ca, cb):
    return lax.dot_general(a, b, (((ca,), (cb,)), ((), ())), preferred_element_type=F32)


def core_swap(x, experts):
    return lax.ppermute(x, "expert", [(i, i ^ 1) for i in range(experts)])


def chip_shift(x, experts, k):
    return lax.ppermute(x, "expert", [((i + 2 * k) % experts, i) for i in range(experts)])


def gather_blocks(x, experts):
    blocks = []
    for k in range(experts // 2):
        mine = x if k == 0 else chip_shift(x, experts, k)
        blocks += [mine, core_swap(mine, experts)]
    return jnp.concatenate(blocks, axis=0)


def return_blocks(x, experts, tok_count):
    chips = experts // 2
    x = x.reshape(chips, 2, tok_count, -1)
    other = core_swap(x[:, 1], experts)
    pair = (x[:, 0].astype(F32) + other.astype(F32)).astype(x.dtype)
    total = pair[0].astype(F32)
    for k in range(1, chips):
        total = total + chip_shift(pair[k], experts, chips - k).astype(F32)
    return total


def on_device(tokens, expert_ids, gate_weights, out_grad, w_gate, w_up, w_down):
    tok_count, pick_width = expert_ids.shape
    experts = lax.axis_size("expert")
    me = lax.axis_index("expert")
    gate_w, up_w, down_w = w_gate[0], w_up[0], w_down[0]

    routing = jnp.concatenate([expert_ids.astype(F32), gate_weights], axis=1)
    routing = gather_blocks(routing, experts)
    x = gather_blocks(tokens, experts)
    og = gather_blocks(out_grad, experts)

    chosen = routing[:, :pick_width] == me.astype(F32)
    weight = jnp.sum(jnp.where(chosen, routing[:, pick_width:], 0.0), axis=1, keepdims=True)

    gate_pre = dot(x, gate_w, 1, 0)
    up_pre = dot(x, up_w, 1, 0)
    sigmoid = jax.nn.sigmoid(gate_pre)
    activated = gate_pre * sigmoid
    hidden = activated * up_pre
    hidden_scaled = (hidden * weight).astype(BF)
    raw = dot(og, down_w, 1, 1)
    gate_sum = jnp.sum(hidden.astype(BF).astype(F32) * raw, axis=1, keepdims=True)
    hidden_grad = raw * weight
    gate_pre_grad = (hidden_grad * up_pre * (sigmoid * (1.0 + gate_pre * (1.0 - sigmoid)))).astype(BF)
    up_pre_grad = (hidden_grad * activated).astype(BF)

    grad_d = dot(hidden_scaled, og, 0, 0).astype(BF)
    grad_g = dot(x, gate_pre_grad, 0, 0).astype(BF)
    grad_u = dot(x, up_pre_grad, 0, 0).astype(BF)
    down_share = lax.psum_scatter(grad_d, "dp", scatter_dimension=1, tiled=True)
    gate_share = lax.psum_scatter(grad_g, "dp", scatter_dimension=0, tiled=True)
    up_share = lax.psum_scatter(grad_u, "dp", scatter_dimension=0, tiled=True)

    input_grad = (dot(gate_pre_grad, gate_w, 1, 1) + dot(up_pre_grad, up_w, 1, 1)).astype(BF)
    token_grads = return_blocks(input_grad, experts, tok_count).astype(BF)
    gate_grads = return_blocks(jnp.where(chosen, gate_sum, 0.0), experts, tok_count)
    return (
        token_grads,
        gate_grads,
        gate_share[None],
        up_share[None],
        down_share[None],
    )


def solution(mesh):
    rows = P(("groups", "expert", "dp"), None)
    weights = P("expert", None, None)
    return jax.shard_map(
        on_device,
        mesh=mesh,
        in_specs=(rows, rows, rows, rows, weights, weights, weights),
        out_specs=(
            rows,
            rows,
            P(("groups", "expert"), "dp", None),
            P(("groups", "expert"), "dp", None),
            P(("groups", "expert"), None, "dp"),
        ),
        check_vma=False,
    )
```

```python
import functools

import jax
import jax.numpy as jnp
from jax import lax
from jax.experimental import pallas as pl
from jax.experimental.pallas import tpu as pltpu
from jax.sharding import PartitionSpec as P

BF = jnp.bfloat16
F32 = jnp.float32
VMEM_SMALL = 28 * 1024 * 1024
VMEM_LARGE = 28 * 1024 * 1024
COST = pl.CostEstimate(flops=1000, bytes_accessed=1000, transcendentals=0)


def dot(a, b, ca, cb):
    return lax.dot_general(a, b, (((ca,), (cb,)), ((), ())), preferred_element_type=F32)


def send(x, axis, pairs, what):
    with jax.named_scope(what):
        return lax.ppermute(x, axis, pairs)


def core_swap(x, experts, what):
    return send(x, "expert", [(i, i ^ 1) for i in range(experts)], what + "_core")


def chip_shift(x, experts, k, what):
    return send(x, "expert", [((i + 2 * k) % experts, i) for i in range(experts)], what + "_chip")


def gather_pairs(x, experts, what):
    pairs = []
    for k in range(experts // 2):
        mine = x if k == 0 else chip_shift(x, experts, k, what)
        pairs.append((mine, core_swap(mine, experts, what)))
    return pairs


def flat(pairs):
    return [b for pair in pairs for b in pair]


def return_sums(pairs, experts, what):
    return [add(own, core_swap(other, experts, what)) for own, other in pairs]


def return_shift(sums, experts, what):
    chips = experts // 2
    return add(sums[0], *(chip_shift(sums[k], experts, chips - k, what) for k in range(1, chips)))


def add(*terms):
    total = terms[0].astype(F32)
    for t in terms[1:]:
        total = total + t.astype(F32)
    return total.astype(terms[0].dtype)


def line_step(x, step, size, towards, what):
    if towards > 0:
        pairs = [(i, i + 1) for i in range(size - 1) if i >= step]
    else:
        pairs = [(i, i - 1) for i in range(1, size) if size - 1 - i >= step]
    return send(x, "dp", pairs, what + ("_right" if towards > 0 else "_left"))


def rotate(x, k, size, what):
    return send(x, "dp", [(i, (i + k) % size) for i in range(size)], what + "_rotated")


def inward(x, size, what):
    return send(x, "dp", [(0, 1), (size - 1, size - 2)], what + "_inward")


def outward(x, size, what):
    return send(x, "dp", [(1, 0), (size - 2, size - 1)], what + "_outward")


def across(x, what):
    return send(x, "dp", [(1, 2), (2, 1)], what + "_across")


def call(body, name, grid, inputs, outputs, scratch=(), deps=(), limit=VMEM_SMALL):
    def spec(entry):
        if len(entry) == 2:
            return pl.BlockSpec(memory_space=entry[1])
        return pl.BlockSpec(entry[1], entry[2])

    n = len(inputs)

    def kernel(*refs):
        body(*refs[:n], *refs[n + len(deps) :])

    return pl.pallas_call(
        kernel,
        grid=grid,
        in_specs=[spec(e) for e in inputs] + [pl.BlockSpec(memory_space=pl.ANY)] * len(deps),
        out_specs=[pl.BlockSpec(o[2], o[3]) for o in outputs],
        out_shape=[jax.ShapeDtypeStruct(o[0], o[1]) for o in outputs],
        scratch_shapes=list(scratch),
        compiler_params=pltpu.CompilerParams(vmem_limit_bytes=limit),
        cost_estimate=COST,
        name=name,
    )(*[e[0] for e in inputs], *deps)


def whole(a):
    return (a, a.shape, lambda *i: (0,) * a.ndim)


def copies(blocks, target, sem, first=0):
    rows = blocks[0].shape[0]
    return [
        pltpu.make_async_copy(b, target.at[pl.ds(i * rows, rows)], sem.at[first + i])
        for i, b in enumerate(blocks)
    ]


def fetch(*args):
    moves = copies(*args)
    for m in moves:
        m.start()
    for m in moves:
        m.wait()


def turned(a, b):
    rows, cols = a.shape
    tile = 512

    def body(a, b, at, bt):
        at[...] = a[...].T
        bt[...] = b[...].T

    inputs = [(x, (tile, cols), lambda i: (i, 0)) for x in (a, b)]
    outputs = [((cols, rows), a.dtype, (cols, tile), lambda i: (0, i))] * 2
    return call(body, "turned", (rows // tile,), inputs, outputs)


def forward(pair, gate_wt, up_wt, deps=()):
    rows, width = 2 * pair[0].shape[0], pair[0].shape[1]
    units = gate_wt.shape[0]
    tile = 256

    def body(a, b, gate_wt, up_wt, hidden, gate_factor, up_factor, x, sem):
        @pl.when(pl.program_id(0) == 0)
        def _():
            fetch((a, b), x, sem)

        gate_pre = dot(gate_wt[...], x[...], 1, 1)
        up_pre = dot(up_wt[...], x[...], 1, 1)
        sigmoid = jax.nn.sigmoid(gate_pre)
        activated = gate_pre * sigmoid
        hidden[...] = (activated * up_pre).astype(BF)
        gate_factor[...] = up_pre * (sigmoid * (1.0 + gate_pre * (1.0 - sigmoid)))
        up_factor[...] = activated

    at = lambda i: (i, 0)
    return call(
        body,
        "forward",
        (units // tile,),
        [(b, pl.ANY) for b in pair] + [(w, (tile, width), at) for w in (gate_wt, up_wt)],
        [((units, rows), t, (tile, rows), at) for t in (BF, F32, F32)],
        [pltpu.VMEM((rows, width), BF), pltpu.SemaphoreType.DMA((2,))],
        deps,
    )


def backward(pair, down_w, weight, hidden, gate_factor, up_factor, deps=()):
    rows, width = 2 * pair[0].shape[0], pair[0].shape[1]
    units = down_w.shape[0]
    tile = 256

    def body(
        a, b, down_w, weight, hidden, gate_factor, up_factor, gate_grad, up_grad, gate_sum, og, sem
    ):
        step = pl.program_id(0)

        @pl.when(step == 0)
        def _():
            fetch((a, b), og, sem)
            gate_sum[...] = jnp.zeros_like(gate_sum)

        raw = dot(down_w[...], og[...], 1, 1)
        scaled = raw * weight[...]
        gate_grad[...] = (scaled * gate_factor[...]).astype(BF)
        up_grad[...] = (scaled * up_factor[...]).astype(BF)
        gate_sum[...] += jnp.sum(raw * hidden[...].astype(F32), axis=0, keepdims=True)

    at = lambda i: (i, 0)
    tall = (tile, rows)
    return call(
        body,
        "backward",
        (units // tile,),
        [(b, pl.ANY) for b in pair]
        + [(down_w, (tile, width), at), whole(weight)]
        + [(a, tall, at) for a in (hidden, gate_factor, up_factor)],
        [((units, rows), BF, tall, at)] * 2 + [((1, rows), F32, (1, rows), lambda i: (0, 0))],
        [pltpu.VMEM((rows, width), BF), pltpu.SemaphoreType.DMA((2,))],
        deps,
        VMEM_LARGE,
    )


def slots(info, me, count):
    pairs, height, rows = info.shape
    width = height // 2

    def body(me, info, table, weight):
        chosen = info[0, :width] == me[0]
        weight[0] = jnp.sum(jnp.where(chosen, info[0, width:], 0.0), axis=0, keepdims=True)
        picked = jnp.sum(jnp.where(chosen, 1.0, 0.0), axis=0, keepdims=True)
        rank = jnp.broadcast_to(picked, (8, rows))
        lane = lax.broadcasted_iota(jnp.int32, (8, rows), 1)
        step = 1
        while step < rows:
            rank = rank + jnp.where(lane >= step, pltpu.roll(rank, step, 1), 0.0)
            step *= 2
        slot = jnp.where(picked > 0.0, rank[:1] - 1.0, float(count)).astype(jnp.int32)
        row = lax.broadcasted_iota(jnp.int32, (count, rows), 0)
        table[0] = jnp.where(row == slot, 1.0, 0.0).astype(BF)

    at = lambda i: (i, 0, 0)
    return call(
        body,
        "slots",
        (pairs,),
        [(me, pltpu.SMEM), (info, (1, height, rows), at)],
        [
            ((pairs, count, rows), BF, (1, count, rows), at),
            ((pairs, 1, rows), F32, (1, 1, rows), at),
        ],
    )


TAGS = 16


def pack(groups, tables, pairs, weight=None, deps=()):
    units, rows = groups[0][0].shape
    count = tables.shape[1]
    n = len(pairs)
    step = 256 if units % 256 == 0 else units
    inputs = [p for g in groups for p in g] + ([] if weight is None else [weight]) + [tables]

    def body(*refs):
        refs, out = refs[:-1], refs[-1]
        for i, c in enumerate(pairs):
            table = refs[-1][c]
            cols = slice(i * count, (i + 1) * count)
            for j in range(len(groups)):
                for start in range(0, units, step):
                    here = refs[j * n + i][start : start + step]
                    if weight is not None:
                        here = (here.astype(F32) * refs[-2][c]).astype(BF)
                    at = j * units + start
                    out[at : at + step, cols] = dot(here, table, 1, 1).astype(BF)
            token = lax.broadcasted_iota(jnp.int32, (TAGS, rows), 1) + c * rows
            row = lax.broadcasted_iota(jnp.int32, (TAGS, rows), 0)
            token = jnp.where(row == 0, token // 256, jnp.where(row == 1, token % 256, 0))
            tags = dot(token.astype(F32).astype(BF), table, 1, 1)
            out[len(groups) * units :, cols] = tags.astype(BF)

    shape = (len(groups) * units + TAGS, n * count)
    return call(
        body,
        "pack",
        (1,),
        [whole(a) for a in inputs],
        [(shape, BF, shape, lambda i: (0, 0))],
        (),
        deps,
        VMEM_LARGE,
    )[0]


def spread(packed, tags, rows, first=0):
    tags = tags.astype(F32)
    token = (tags[:1] * 256.0 + tags[1:2]).astype(jnp.int32) - first
    row = lax.broadcasted_iota(jnp.int32, (rows, packed.shape[1]), 0)
    table = jnp.where(row == token, 1.0, 0.0).astype(BF)
    return dot(packed, table, 1, 1).astype(BF)


def sum_products(packed, valid, blocks, order, parts, deps=()):
    height, width = blocks[0].shape
    rows, share = height * len(blocks), width // parts
    units = packed[0].shape[0] - TAGS
    m, n = len(packed), len(blocks)

    def body(valid, *refs):
        blocks, packed, (out, total, whole_rows, sem) = refs[:n], refs[n : n + m], refs[n + m :]
        fetch(blocks, whole_rows, sem)
        total[...] = jnp.zeros_like(total)
        for i in range(m):

            @pl.when(valid[i] > 0)
            def _():
                left = spread(packed[i][:units], packed[i][units:], rows)
                cols = slice(order[i] * share, (order[i] + 1) * share)
                total[...] += dot(left, whole_rows[:, cols], 1, 0)

        out[...] = total[...].astype(BF)

    return call(
        body,
        "sum_products",
        (1,),
        [(valid, pltpu.SMEM)] + [(b, pl.ANY) for b in blocks] + [whole(a) for a in packed],
        [((units, share), BF, (units, share), lambda i: (0, 0))],
        [
            pltpu.VMEM((units, share), F32),
            pltpu.VMEM((rows, width), BF),
            pltpu.SemaphoreType.DMA((n,)),
        ],
        deps,
        VMEM_LARGE,
    )[0]


def input_grad(gate_grad, up_grad, gate_wt, up_wt, sums, deps=()):
    units, rows = gate_grad.shape
    width = gate_wt.shape[1]
    tile = 512
    half = rows // 2
    picks = sums.shape[0]

    def body(gate_grad, up_grad, gate_wt, up_wt, sums, own, other, g, u):
        @pl.when(pl.program_id(0) == 0)
        def _():
            g[...] = gate_grad[...].T
            u[...] = up_grad[...].T

        total = dot(g[...], gate_wt[...], 1, 0) + dot(u[...], up_wt[...], 1, 0)
        for i, out in enumerate((own, other)):
            out[:half] = total[i * half : (i + 1) * half].astype(BF)
            out[half:] = jnp.zeros((TAGS, tile), BF)

            @pl.when(pl.program_id(0) == 0)
            def _():
                left = sums[:, i * half : (i + 1) * half]
                parts = []
                for _ in range(3):
                    parts.append(left.astype(BF).astype(F32))
                    left = left - parts[-1]
                parts.append(jnp.zeros((TAGS - 3 * picks, half), F32))
                out[half:, :half] = jnp.concatenate(parts, axis=0).astype(BF)

    at = lambda i: (0, i)
    return call(
        body,
        "input_grad",
        (width // tile,),
        [whole(gate_grad), whole(up_grad)]
        + [(w, (units, tile), at) for w in (gate_wt, up_wt)]
        + [whole(sums)],
        [((half + TAGS, width), BF, (half + TAGS, tile), at)] * 2,
        [pltpu.VMEM((rows, units), BF)] * 2,
        deps,
        VMEM_LARGE,
    )


def weight_grad(x_pairs, grads, shares, replicas, fold=None, deps=()):
    chips = len(x_pairs)
    blocks = flat(x_pairs)
    small = list(grads)
    units, rows = grads[0].shape
    width = blocks[0].shape[1]
    if fold is not None:
        blocks = blocks + flat(fold[0])
        small = small + [fold[1]]
    total = len(blocks) * blocks[0].shape[0]
    share = width // replicas

    def body(shares, *refs):
        blocks_in, refs = refs[: len(blocks)], refs[len(blocks) :]
        small_in, (out, x, g, sem) = refs[: len(small)], refs[len(small) :]
        step = pl.program_id(0)

        @pl.when(step == 0)
        def _():
            moves = copies(blocks_in, x, sem)
            for m in moves:
                m.start()
            for i in range(chips):
                g[:, i * rows : (i + 1) * rows] = small_in[i][...]
            if fold is not None:
                packed = small_in[chips]
                for i in range(chips):
                    part = slice(i * packed.shape[1] // chips, (i + 1) * packed.shape[1] // chips)
                    at = (chips + i) * rows
                    g[:, at : at + rows] = spread(
                        packed[:units, part], packed[units:, part], rows, i * rows
                    )
            for m in moves:
                m.wait()

        cols = pl.ds(pl.multiple_of(shares[step] * share, share), share)
        out[0] = dot(g[...], x[:, cols], 1, 0).astype(BF)

    n = shares.shape[0]
    return call(
        body,
        "weight_grad",
        (n,),
        [(shares, pltpu.SMEM)] + [(b, pl.ANY) for b in blocks] + [whole(a) for a in small],
        [((n, units, share), BF, (1, units, share), lambda i: (i, 0, 0))],
        [
            pltpu.VMEM((total, width), BF),
            pltpu.VMEM((units, total), BF),
            pltpu.SemaphoreType.DMA((len(blocks),)),
        ],
        deps,
        VMEM_LARGE,
    )[0]


def on_device(tokens, expert_ids, gate_weights, out_grad, w_gate, w_up, w_down):
    tok_count, pick_width = expert_ids.shape
    experts, replicas = lax.axis_size("expert"), lax.axis_size("dp")
    chips = experts // 2
    me, z = lax.axis_index("expert").astype(F32).reshape(1), lax.axis_index("dp")
    down_w = w_down[0]
    width = tokens.shape[1]
    share = width // replicas
    capacity = 4 * tok_count * pick_width // (3 * experts)
    count = experts * capacity
    pair_rows = 2 * tok_count
    folding = replicas == 4
    pairs = list(range(chips))
    meet = lax.optimization_barrier

    x_core = core_swap(tokens, experts, "tokens")
    x_fold = inward(tokens, replicas, "tokens") if folding else tokens
    x_far = [chip_shift(tokens, experts, k, "tokens") for k in range(1, chips)]
    info = jnp.concatenate([expert_ids.T.astype(F32), gate_weights.T], axis=0)
    info_far = [chip_shift(info, experts, k, "routing") for k in range(1, chips)]
    og_shares = []
    for k in range(replicas):
        part = lax.dynamic_slice_in_dim(out_grad, (z + k) % replicas * share, share, 1)
        og_shares.append(rotate(part, k, replicas, "out_grad_share") if k else part)
    gate_wt, up_wt = turned(w_gate[0], w_up[0])
    fwd = [forward((tokens, x_core), gate_wt, up_wt)]
    x_far, info, info_far, x_fold, out_grad, gate_wt, up_wt, fwd = meet(
        (x_far, info, info_far, x_fold, out_grad, gate_wt, up_wt, fwd)
    )

    og_core = core_swap(out_grad, experts, "out_grad")
    og_far = [chip_shift(out_grad, experts, k, "out_grad") for k in range(1, chips)]
    x = [(tokens, x_core)] + [(b, core_swap(b, experts, "tokens")) for b in x_far]
    info = [(b, core_swap(b, experts, "routing")) for b in (info, *info_far)]
    info = jnp.stack([jnp.concatenate(pair, axis=1) for pair in info])
    fwd += [forward(pair, gate_wt, up_wt) for pair in x[1:]]
    tables, weights = slots(info, me, count // chips)
    packed = pack([[f[0] for f in fwd]], tables, pairs, weights)
    right = [line_step(packed, 0, replicas, 1, "hidden")]
    left = [line_step(packed, 0, replicas, -1, "hidden")]
    og_far, og_core, og_shares, fwd, tables, weights, x, x_fold, info = meet(
        (og_far, og_core, og_shares, fwd, tables, weights, x, x_fold, info)
    )

    def onward(t):
        right.append(line_step(right[-1], t, replicas, 1, "hidden"))
        left.append(line_step(left[-1], t, replicas, -1, "hidden"))

    bwd = [backward((out_grad, og_core), down_w, weights[0], *fwd[0])]
    for c in range(1, chips):
        pair = (og_far[c - 1], core_swap(og_far[c - 1], experts, "out_grad"))
        bwd.append(backward(pair, down_w, weights[c], *fwd[c]))
    gate_grad, up_grad = [b[0] for b in bwd], [b[1] for b in bwd]
    og_rows = jnp.concatenate(og_shares, axis=1)

    def input_grads(deps=()):
        halves = []
        for c, (gate, up, sums) in enumerate(bwd):
            sums = jnp.where(info[c, :pick_width] == me, sums, 0.0)
            halves.append(input_grad(gate, up, gate_wt, up_wt, sums, deps))
        return halves

    def grad_down(og_rows):
        gathered, blocks, valid = [packed], [0], [z >= 0]
        for t in range(replicas - 1):
            gathered += [right[t], left[t]]
            blocks += [t + 1, replicas - 1 - t]
            valid += [z - 1 - t >= 0, z + 1 + t < replicas]
        valid = jnp.stack(valid).astype(jnp.int32)
        return sum_products(gathered, valid, flat(og_rows), blocks, replicas)

    if folding:
        x_there = [chip_shift(x_fold, experts, k, "tokens_fold") for k in range(1, chips)]
        gate_packed = pack([gate_grad], tables, pairs)
        up_packed = pack([up_grad], tables, pairs, None, [gate_packed])
        gate_there = inward(gate_packed, replicas, "gate_grad")
        up_there = inward(up_packed, replicas, "up_grad")
        right, left, bwd, gate_grad, up_grad, og_rows, x_there = meet(
            (right, left, bwd, gate_grad, up_grad, og_rows, x_there)
        )

        onward(1)
        x_there = [(b, core_swap(b, experts, "tokens_fold")) for b in [x_fold, *x_there]]
        og_rows = [og_rows, *(chip_shift(og_rows, experts, k, "out_grad_share") for k in range(1, chips))]
        gate_there, x_there, gate_grad = meet((gate_there, x_there, gate_grad))

        order = jnp.where(z < 2, jnp.arange(3, -1, -1), jnp.arange(4)).astype(jnp.int32)
        gate_sent = weight_grad(x, gate_grad, order[:2], replicas, (x_there, gate_there))
        gate_met = across(gate_sent, "gate_sums")
        og_rows = [(b, core_swap(b, experts, "out_grad_share")) for b in og_rows]
        up_there, gate_sent, gate_there, x_there, gate_grad, up_grad, right, left = meet(
            (up_there, gate_sent, gate_there, x_there, gate_grad, up_grad, right, left)
        )

        up_sent = weight_grad(x, up_grad, order[:2], replicas, (x_there, up_there))
        up_met = [across(up_sent[0], "up_far_sums"), across(up_sent[1], "up_sums")]
        gate_kept = weight_grad(x, gate_grad, order[2:], replicas, (x_there, gate_there), [up_sent])
        up_kept = weight_grad(x, up_grad, order[2:], replicas, (x_there, up_there), [gate_kept])
        onward(2)
        halves = input_grads([up_kept])
        gate_met, gate_kept, up_kept, halves, og_rows, right, left = meet(
            (gate_met, gate_kept, up_kept, halves, og_rows, right, left)
        )

        gate_far = outward(add(gate_kept[1], gate_met[0]).T, replicas, "gate_sums")
        gate_own = add(gate_kept[0], gate_met[1]).T
        sums = return_sums(halves, experts, "token_grads")
        down = grad_down(og_rows)
        up_met[0], up_kept, gate_own, sums, down = meet(
            (up_met[0], up_kept, gate_own, sums, down)
        )

        outer = (z == 0) | (z == replicas - 1)
        up_far = outward(add(up_kept[1], up_met[0]).T, replicas, "up_sums")
        grads = return_shift(sums, experts, "token_grads")
        gate_share = jnp.where(outer, gate_far, gate_own)
        up_share = jnp.where(outer, up_far, add(up_kept[0], up_met[1]).T)
    else:
        every = jnp.arange(replicas, dtype=jnp.int32)

        def scatter(grads):
            total = weight_grad(x, grads, every, replicas)
            return lax.psum_scatter(total, "dp", scatter_dimension=0, tiled=True)[0].T

        gate_share, up_share = scatter(gate_grad), scatter(up_grad)
        for t in range(1, replicas - 1):
            onward(t)
        grads = return_shift(return_sums(input_grads(), experts, "token_grads"), experts, "token_grads")
        down = grad_down(gather_pairs(og_rows, experts, "out_grad_share"))
    token_grads = grads[:tok_count]
    sums = grads[tok_count:, :tok_count].astype(F32)
    gate_grads = sum(sums[i * pick_width : (i + 1) * pick_width] for i in range(3)).T
    return (
        token_grads,
        gate_grads,
        gate_share[None],
        up_share[None],
        down[None],
    )


def solution(mesh):
    rows = P(("groups", "expert", "dp"), None)
    weights = P("expert", None, None)
    return jax.shard_map(
        on_device,
        mesh=mesh,
        in_specs=(rows, rows, rows, rows, weights, weights, weights),
        out_specs=(
            rows,
            rows,
            P(("groups", "expert"), "dp", None),
            P(("groups", "expert"), "dp", None),
            P(("groups", "expert"), None, "dp"),
        ),
        check_vma=False,
    )
```

```python
import functools

import jax
import jax.numpy as jnp
from jax import lax
from jax.experimental import pallas as pl
from jax.experimental.pallas import tpu as pltpu
from jax.sharding import PartitionSpec as P

BF = jnp.bfloat16
F32 = jnp.float32
VMEM_SMALL = 28 * 1024 * 1024
VMEM_LARGE = 60 * 1024 * 1024
COST = pl.CostEstimate(flops=1000, bytes_accessed=1000, transcendentals=0)


def dot(a, b, ca, cb):
    return lax.dot_general(a, b, (((ca,), (cb,)), ((), ())), preferred_element_type=F32)


def send(x, axis, pairs, what):
    with jax.named_scope(what):
        return lax.ppermute(x, axis, pairs)


def core_swap(x, experts, what):
    return send(x, "expert", [(i, i ^ 1) for i in range(experts)], what + "_core")


def chip_shift(x, experts, k, what):
    return send(x, "expert", [((i + 2 * k) % experts, i) for i in range(experts)], what + "_chip")


def gather_pairs(x, experts, what):
    pairs = []
    for k in range(experts // 2):
        mine = x if k == 0 else chip_shift(x, experts, k, what)
        pairs.append((mine, core_swap(mine, experts, what)))
    return pairs


def flat(pairs):
    return [b for pair in pairs for b in pair]


def return_sums(pairs, experts, what):
    return [add(own, core_swap(other, experts, what)) for own, other in pairs]


def add(*terms):
    total = terms[0].astype(F32)
    for t in terms[1:]:
        total = total + t.astype(F32)
    return total.astype(terms[0].dtype)


def line_step(x, step, size, towards, what):
    if towards > 0:
        pairs = [(i, i + 1) for i in range(size - 1) if i >= step]
    else:
        pairs = [(i, i - 1) for i in range(1, size) if size - 1 - i >= step]
    return send(x, "dp", pairs, what + ("_right" if towards > 0 else "_left"))


def rotate(x, k, size, what):
    return send(x, "dp", [(i, (i + k) % size) for i in range(size)], what + "_rotated")


def inward(x, size, what):
    return send(x, "dp", [(0, 1), (size - 1, size - 2)], what + "_inward")


def outward(x, size, what):
    return send(x, "dp", [(1, 0), (size - 2, size - 1)], what + "_outward")


def across(x, what):
    return send(x, "dp", [(1, 2), (2, 1)], what + "_across")


def call(body, name, grid, inputs, outputs, scratch=(), deps=(), limit=VMEM_SMALL):
    def spec(entry):
        if len(entry) == 2:
            return pl.BlockSpec(memory_space=entry[1])
        return pl.BlockSpec(entry[1], entry[2])

    n = len(inputs)

    def kernel(*refs):
        body(*refs[:n], *refs[n + len(deps) :])

    return pl.pallas_call(
        kernel,
        grid=grid,
        in_specs=[spec(e) for e in inputs] + [pl.BlockSpec(memory_space=pl.ANY)] * len(deps),
        out_specs=[pl.BlockSpec(o[2], o[3]) for o in outputs],
        out_shape=[jax.ShapeDtypeStruct(o[0], o[1]) for o in outputs],
        scratch_shapes=list(scratch),
        compiler_params=pltpu.CompilerParams(vmem_limit_bytes=limit),
        cost_estimate=COST,
        name=name,
    )(*[e[0] for e in inputs], *deps)


def whole(a):
    return (a, a.shape, lambda *i: (0,) * a.ndim)


def copies(blocks, target, sem, first=0, axis=0):
    size = blocks[0].shape[axis]
    moves = []
    for i, b in enumerate(blocks):
        at = pl.ds(i * size, size)
        part = target.at[at] if axis == 0 else target.at[:, at]
        moves.append(pltpu.make_async_copy(b, part, sem.at[first + i]))
    return moves


def fetch(*args):
    moves = copies(*args)
    for m in moves:
        m.start()
    for m in moves:
        m.wait()


def turned(a, b):
    rows, cols = a.shape
    tile = 512

    def body(a, b, at, bt):
        at[...] = a[...].T
        bt[...] = b[...].T

    inputs = [(x, (tile, cols), lambda i: (i, 0)) for x in (a, b)]
    outputs = [((cols, rows), a.dtype, (cols, tile), lambda i: (0, i))] * 2
    return call(body, "turned", (rows // tile,), inputs, outputs)


def forward(pair, gate_wt, up_wt, deps=()):
    rows, width = 2 * pair[0].shape[0], pair[0].shape[1]
    units = gate_wt.shape[0]
    tile = 256

    def body(a, b, gate_wt, up_wt, hidden, gate_factor, up_factor, x, sem):
        @pl.when(pl.program_id(0) == 0)
        def _():
            fetch((a, b), x, sem)

        gate_pre = dot(gate_wt[...], x[...], 1, 1)
        up_pre = dot(up_wt[...], x[...], 1, 1)
        sigmoid = jax.nn.sigmoid(gate_pre)
        activated = gate_pre * sigmoid
        hidden[...] = (activated * up_pre).astype(BF)
        gate_factor[...] = (up_pre * (sigmoid * (1.0 + gate_pre * (1.0 - sigmoid)))).astype(BF)
        up_factor[...] = activated.astype(BF)

    at = lambda i: (i, 0)
    return call(
        body,
        "forward",
        (units // tile,),
        [(b, pltpu.HBM) for b in pair] + [(w, (tile, width), at) for w in (gate_wt, up_wt)],
        [((units, rows), t, (tile, rows), at) for t in (BF, BF, BF)],
        [pltpu.VMEM((rows, width), BF), pltpu.SemaphoreType.DMA((2,))],
        deps,
    )


def backward(pair, down_w, weight, hidden, gate_factor, up_factor, deps=()):
    rows, width = 2 * pair[0].shape[0], pair[0].shape[1]
    units = down_w.shape[0]
    tile = 256

    def body(
        a, b, down_w, weight, hidden, gate_factor, up_factor, gate_grad, up_grad, gate_sum, og, sem
    ):
        step = pl.program_id(0)

        @pl.when(step == 0)
        def _():
            fetch((a, b), og, sem)
            gate_sum[...] = jnp.zeros_like(gate_sum)

        raw = dot(down_w[...], og[...], 1, 1)
        scaled = raw * weight[...]
        gate_grad[...] = (scaled * gate_factor[...].astype(F32)).astype(BF)
        up_grad[...] = (scaled * up_factor[...].astype(F32)).astype(BF)
        gate_sum[...] += jnp.sum(raw * hidden[...].astype(F32), axis=0, keepdims=True)

    at = lambda i: (i, 0)
    tall = (tile, rows)
    return call(
        body,
        "backward",
        (units // tile,),
        [(b, pltpu.HBM) for b in pair]
        + [(down_w, (tile, width), at), whole(weight)]
        + [(a, tall, at) for a in (hidden, gate_factor, up_factor)],
        [((units, rows), BF, tall, at)] * 2 + [((1, rows), F32, (1, rows), lambda i: (0, 0))],
        [pltpu.VMEM((rows, width), BF), pltpu.SemaphoreType.DMA((2,))],
        deps,
    )


def slots(info, me, count):
    pairs, height, rows = info.shape
    width = height // 2

    def body(me, info, table, weight):
        chosen = info[0, :width] == me[0]
        weight[0] = jnp.sum(jnp.where(chosen, info[0, width:], 0.0), axis=0, keepdims=True)
        picked = jnp.sum(jnp.where(chosen, 1.0, 0.0), axis=0, keepdims=True)
        rank = jnp.broadcast_to(picked, (8, rows))
        lane = lax.broadcasted_iota(jnp.int32, (8, rows), 1)
        step = 1
        while step < rows:
            rank = rank + jnp.where(lane >= step, pltpu.roll(rank, step, 1), 0.0)
            step *= 2
        slot = jnp.where(picked > 0.0, rank[:1] - 1.0, float(count)).astype(jnp.int32)
        row = lax.broadcasted_iota(jnp.int32, (count, rows), 0)
        table[0] = jnp.where(row == slot, 1.0, 0.0).astype(BF)

    at = lambda i: (i, 0, 0)
    return call(
        body,
        "slots",
        (pairs,),
        [(me, pltpu.SMEM), (info, (1, height, rows), at)],
        [
            ((pairs, count, rows), BF, (1, count, rows), at),
            ((pairs, 1, rows), F32, (1, 1, rows), at),
        ],
    )


TAGS = 16


def pack(groups, tables, pairs, weight=None, deps=()):
    units, rows = groups[0][0].shape
    count = tables.shape[1]
    n = len(pairs)
    step = 256 if units % 256 == 0 else units
    inputs = [p for g in groups for p in g] + ([] if weight is None else [weight]) + [tables]

    def body(*refs):
        refs, outs = refs[: len(inputs)], refs[len(inputs) :]
        for i, c in enumerate(pairs):
            table = refs[-1][c]
            cols = slice(i * count, (i + 1) * count)
            for j in range(len(groups)):
                for start in range(0, units, step):
                    here = refs[j * n + i][start : start + step]
                    if weight is not None:
                        here = (here.astype(F32) * refs[-2][c]).astype(BF)
                    outs[j][start : start + step, cols] = dot(here, table, 1, 1).astype(BF)
            token = lax.broadcasted_iota(jnp.int32, (TAGS, rows), 1) + c * rows
            row = lax.broadcasted_iota(jnp.int32, (TAGS, rows), 0)
            token = jnp.where(row == 0, token // 256, jnp.where(row == 1, token % 256, 0))
            tags = dot(token.astype(F32).astype(BF), table, 1, 1)
            for out in outs:
                out[units:, cols] = tags.astype(BF)

    shape = (units + TAGS, n * count)
    return call(
        body,
        "pack",
        (1,),
        [whole(a) for a in inputs],
        [(shape, BF, shape, lambda i: (0, 0))] * len(groups),
        (),
        deps,
    )


def spread(packed, tags, rows, first=0):
    tags = tags.astype(F32)
    token = (tags[:1] * 256.0 + tags[1:2]).astype(jnp.int32) - first
    row = lax.broadcasted_iota(jnp.int32, (rows, packed.shape[1]), 0)
    table = jnp.where(row == token, 1.0, 0.0).astype(BF)
    return dot(packed, table, 1, 1).astype(BF)


def sum_products(packed, valid, blocks, order, parts, deps=()):
    height, width = blocks[0].shape
    rows, share = height * len(blocks), width // parts
    units = packed[0].shape[0] - TAGS
    m, n = len(packed), len(blocks)

    def body(valid, *refs):
        blocks, packed, (out, total, whole_rows, held, sem) = refs[:n], refs[n : n + m], refs[n + m :]
        moves = copies(blocks, whole_rows, sem)
        for move in moves:
            move.start()
        arrivals = [
            pltpu.make_async_copy(packed[i], held.at[i], sem.at[n + i]) for i in range(m)
        ]
        for move in arrivals:
            move.start()
        total[...] = jnp.zeros_like(total)
        for move in moves:
            move.wait()
        for i in range(m):
            arrivals[i].wait()

            @pl.when(valid[i] > 0)
            def _():
                left = spread(held[i, :units], held[i, units:], rows)
                cols = slice(order[i] * share, (order[i] + 1) * share)
                total[...] += dot(left, whole_rows[:, cols], 1, 0)

        out[...] = total[...].astype(BF)

    return call(
        body,
        "sum_products",
        (1,),
        [(valid, pltpu.SMEM)] + [(a, pltpu.HBM) for a in (*blocks, *packed)],
        [((units, share), BF, (units, share), lambda i: (0, 0))],
        [
            pltpu.VMEM((units, share), F32),
            pltpu.VMEM((rows, width), BF),
            pltpu.VMEM((m, *packed[0].shape), BF),
            pltpu.SemaphoreType.DMA((n + m,)),
        ],
        deps,
        VMEM_LARGE,
    )[0]


def input_grad(gate_grads, up_grads, gate_wt, up_wt, sums, deps=()):
    units, rows = gate_grads[0].shape
    width = gate_wt.shape[1]
    tile = 512
    half = rows // 2
    chips = len(gate_grads)
    picks = sums[0].shape[0]

    def body(*refs):
        grads, (gate_wt, up_wt), refs = refs[: 2 * chips], refs[2 * chips : 2 * chips + 2], refs[2 * chips + 2 :]
        sums, outs, turned = refs[:chips], refs[chips : 3 * chips], refs[3 * chips :]
        step = pl.program_id(0)

        @pl.when(step == 0)
        def _():
            for a, b in zip(grads, turned):
                b[...] = a[...].T

        for c in range(chips):
            total = dot(turned[c][...], gate_wt[...], 1, 0)
            total = total + dot(turned[chips + c][...], up_wt[...], 1, 0)
            for i in range(2):
                out = outs[2 * c + i]
                out[:half] = total[i * half : (i + 1) * half].astype(BF)
                out[half:] = jnp.zeros((TAGS, tile), BF)

                @pl.when(step == 0)
                def _():
                    left = sums[c][:, i * half : (i + 1) * half]
                    parts = []
                    for _ in range(3):
                        parts.append(left.astype(BF).astype(F32))
                        left = left - parts[-1]
                    parts.append(jnp.zeros((TAGS - 3 * picks, half), F32))
                    out[half:, :half] = jnp.concatenate(parts, axis=0).astype(BF)

    at = lambda i: (0, i)
    outs = call(
        body,
        "input_grad",
        (width // tile,),
        [whole(a) for a in (*gate_grads, *up_grads)]
        + [(w, (units, tile), at) for w in (gate_wt, up_wt)]
        + [whole(a) for a in sums],
        [((half + TAGS, width), BF, (half + TAGS, tile), at)] * (2 * chips),
        [pltpu.VMEM((rows, units), BF)] * (2 * chips),
        deps,
        VMEM_LARGE,
    )
    return [(outs[2 * c], outs[2 * c + 1]) for c in range(chips)]


def finish_tokens(sums, experts, tok_count, picks, deps=()):
    chips = experts // 2
    moved = [chip_shift(sums[k], experts, chips - k, "token_grads") for k in range(1, chips)]
    width = sums[0].shape[1]

    def body(*refs):
        refs, (grads, out) = refs[:chips], refs[chips:]
        total = refs[0][...].astype(F32)
        for ref in refs[1:]:
            total = total + ref[...].astype(F32)
        grads[...] = total[:tok_count].astype(BF)
        parts = total[tok_count:, :tok_count]
        out[...] = parts[:picks] + parts[picks : 2 * picks] + parts[2 * picks : 3 * picks]

    at = lambda i: (0, 0)
    grads, sums = call(
        body,
        "finish_tokens",
        (1,),
        [whole(a) for a in (sums[0], *moved)],
        [((tok_count, width), BF, (tok_count, width), at), ((picks, tok_count), F32, (picks, tok_count), at)],
        (),
        deps,
    )
    return grads, sums.T


def choose(flag, a, b, deps=()):
    def body(flag, a, b, out):
        out[0] = jnp.where(flag[0] > 0, a[...], b[...])

    return call(
        body,
        "choose",
        (1,),
        [(flag, pltpu.SMEM), whole(a), whole(b)],
        [((1, *a.shape), BF, (1, *a.shape), lambda i: (0, 0, 0))],
        (),
        deps,
    )[0]


def weight_grad(x_pairs, grads, shares, replicas, fold=None, deps=(), joined=False, space=pltpu.HBM):
    chips, n = len(x_pairs), shares.shape[0]
    blocks = flat(x_pairs)
    units, rows = grads[0].shape
    width = blocks[0].shape[1]
    packed = []
    if fold is not None:
        blocks = blocks + flat(fold[0])
        packed = [fold[1]]
    total = len(blocks) * blocks[0].shape[0]
    share = width // replicas

    def body(shares, *refs):
        blocks_in, refs = refs[: len(blocks)], refs[len(blocks) :]
        grads_in, refs = refs[:chips], refs[chips:]
        packed_in, refs = refs[: len(packed)], refs[len(packed) :]
        outs, (x, g, sem) = refs[:-3], refs[-3:]
        step = pl.program_id(0)

        @pl.when(step == 0)
        def _():
            moves = copies(blocks_in, x, sem, chips)
            if not joined:
                moves = copies(grads_in, g, sem, 0, 1) + moves
            for m in moves:
                m.start()
            if joined:
                for i in range(chips):
                    g[:, i * rows : (i + 1) * rows] = grads_in[i][...]
            for packed in packed_in:
                for i in range(chips):
                    part = slice(i * packed.shape[1] // chips, (i + 1) * packed.shape[1] // chips)
                    at = (chips + i) * rows
                    g[:, at : at + rows] = spread(
                        packed[:units, part], packed[units:, part], rows, i * rows
                    )
            for m in moves:
                m.wait()

        cols = pl.ds(pl.multiple_of(shares[step] * share, share), share)
        value = dot(g[...], x[:, cols], 1, 0).astype(BF)
        if joined:
            outs[0][0] = value
        else:
            for i, out in enumerate(outs):

                @pl.when(step == i)
                def _():
                    out[...] = value

    if joined:
        outputs = [((n, units, share), BF, (1, units, share), lambda i: (i, 0, 0))]
    else:
        outputs = [((units, share), BF, (units, share), lambda i: (0, 0))] * n
    return call(
        body,
        "weight_grad",
        (n,),
        [(shares, pltpu.SMEM)]
        + [(b, space) for b in blocks]
        + [whole(a) if joined else (a, space) for a in grads]
        + [whole(a) for a in packed],
        outputs,
        [
            pltpu.VMEM((total, width), BF),
            pltpu.VMEM((units, total), BF),
            pltpu.SemaphoreType.DMA((len(blocks) + chips,)),
        ],
        deps,
        VMEM_LARGE,
    )


def turned_sum(a, b, part, deps=()):
    def body(a, b, out):
        out[...] = (a[...].astype(F32) + b[0].astype(F32)).T.astype(BF)

    shape = (a.shape[1], a.shape[0])
    return call(
        body,
        "turned_sum",
        (1,),
        [whole(a), (b, (1, *a.shape), lambda i: (part, 0, 0))],
        [(shape, BF, shape, lambda i: (0, 0))],
        (),
        deps,
    )[0]


def on_device(tokens, expert_ids, gate_weights, out_grad, w_gate, w_up, w_down):
    tok_count, pick_width = expert_ids.shape
    experts, replicas = lax.axis_size("expert"), lax.axis_size("dp")
    chips = experts // 2
    me, z = lax.axis_index("expert").astype(F32).reshape(1), lax.axis_index("dp")
    down_w = w_down[0]
    width = tokens.shape[1]
    share = width // replicas
    capacity = 4 * tok_count * pick_width // (3 * experts)
    count = experts * capacity
    pair_rows = 2 * tok_count
    folding = replicas == 4
    pairs = list(range(chips))
    meet = lax.optimization_barrier

    x_core = core_swap(tokens, experts, "tokens")
    x_fold = inward(tokens, replicas, "tokens") if folding else tokens
    x_far = [chip_shift(tokens, experts, k, "tokens") for k in range(1, chips)]
    info = jnp.concatenate([expert_ids.T.astype(F32), gate_weights.T], axis=0)
    info_far = [chip_shift(info, experts, k, "routing") for k in range(1, chips)]
    og_shares = []
    for k in range(replicas):
        part = lax.dynamic_slice_in_dim(out_grad, (z + k) % replicas * share, share, 1)
        og_shares.append(rotate(part, k, replicas, "out_grad_share") if k else part)
    gate_wt, up_wt = turned(w_gate[0], w_up[0])
    fwd = [forward((tokens, x_core), gate_wt, up_wt)]
    x_far, info, info_far, x_fold, out_grad, gate_wt, up_wt, fwd = meet(
        (x_far, info, info_far, x_fold, out_grad, gate_wt, up_wt, fwd)
    )

    og_core = core_swap(out_grad, experts, "out_grad")
    og_far = [chip_shift(out_grad, experts, k, "out_grad") for k in range(1, chips)]
    x = [(tokens, x_core)] + [(b, core_swap(b, experts, "tokens")) for b in x_far]
    info = [(b, core_swap(b, experts, "routing")) for b in (info, *info_far)]
    info = jnp.stack([jnp.concatenate(pair, axis=1) for pair in info])
    fwd += [forward(pair, gate_wt, up_wt) for pair in x[1:]]
    tables, weights = slots(info, me, count // chips)
    packed = pack([[f[0] for f in fwd]], tables, pairs, weights)[0]
    right = [line_step(packed, 0, replicas, 1, "hidden")]
    left = [line_step(packed, 0, replicas, -1, "hidden")]
    og_far, og_core, og_shares, fwd, tables, weights, x, x_fold, info = meet(
        (og_far, og_core, og_shares, fwd, tables, weights, x, x_fold, info)
    )

    def onward(t):
        right.append(line_step(right[-1], t, replicas, 1, "hidden"))
        left.append(line_step(left[-1], t, replicas, -1, "hidden"))

    bwd = [backward((out_grad, og_core), down_w, weights[0], *fwd[0])]
    for c in range(1, chips):
        pair = (og_far[c - 1], core_swap(og_far[c - 1], experts, "out_grad"))
        bwd.append(backward(pair, down_w, weights[c], *fwd[c]))
    gate_grad, up_grad = [b[0] for b in bwd], [b[1] for b in bwd]
    og_rows = jnp.concatenate(og_shares, axis=1)

    def input_grads(deps=()):
        sums = [jnp.where(info[c, :pick_width] == me, b[2], 0.0) for c, b in enumerate(bwd)]
        return input_grad([b[0] for b in bwd], [b[1] for b in bwd], gate_wt, up_wt, sums, deps)

    def grad_down(og_rows, deps=()):
        gathered, blocks, valid = [packed], [0], [z >= 0]
        for t in range(replicas - 1):
            gathered += [right[t], left[t]]
            blocks += [t + 1, replicas - 1 - t]
            valid += [z - 1 - t >= 0, z + 1 + t < replicas]
        valid = jnp.stack(valid).astype(jnp.int32)
        return sum_products(gathered, valid, flat(og_rows), blocks, replicas, deps)

    if folding:
        x_there = [chip_shift(x_fold, experts, k, "tokens_fold") for k in range(1, chips)]
        gate_packed, up_packed = pack([gate_grad, up_grad], tables, pairs)
        gate_there = inward(gate_packed, replicas, "gate_grad")
        up_there = inward(up_packed, replicas, "up_grad")
        right, left, bwd, gate_grad, up_grad, og_rows, x_there = meet(
            (right, left, bwd, gate_grad, up_grad, og_rows, x_there)
        )

        onward(1)
        x_there = [(b, core_swap(b, experts, "tokens_fold")) for b in [x_fold, *x_there]]
        og_rows = [og_rows, *(chip_shift(og_rows, experts, k, "out_grad_share") for k in range(1, chips))]
        gate_there, x_there, gate_grad = meet((gate_there, x_there, gate_grad))

        order = jnp.where(z < 2, jnp.arange(3, -1, -1), jnp.arange(4)).astype(jnp.int32)
        fold = (x_there, gate_there)
        gate_sent = weight_grad(x, gate_grad, order[:2], replicas, fold, (), True, pl.ANY)[0]
        gate_met = across(gate_sent, "gate_sums")
        og_rows = [(b, core_swap(b, experts, "out_grad_share")) for b in og_rows]
        up_there, gate_sent, gate_there, x_there, gate_grad, up_grad, right, left = meet(
            (up_there, gate_sent, gate_there, x_there, gate_grad, up_grad, right, left)
        )

        up_sent = weight_grad(x, up_grad, order[:2], replicas, (x_there, up_there))
        up_met = [across(up_sent[0], "up_far_sums"), across(up_sent[1], "up_sums")]
        gate_kept = weight_grad(x, gate_grad, order[2:], replicas, (x_there, gate_there), up_sent)
        onward(2)
        halves = input_grads(gate_kept)
        gate_met, gate_kept, up_grad, halves, og_rows, right, left = meet(
            (gate_met, gate_kept, up_grad, halves, og_rows, right, left)
        )
        up_kept = weight_grad(x, up_grad, order[2:], replicas, (x_there, up_there))

        gate_far = outward(turned_sum(gate_kept[1], gate_met, 0), replicas, "gate_sums")
        sums = return_sums(halves, experts, "token_grads")
        gate_own = turned_sum(gate_kept[0], gate_met, 1, up_kept)
        up_met[0], up_kept, sums, gate_own, gate_far = meet(
            (up_met[0], up_kept, sums, gate_own, gate_far)
        )

        outer = ((z == 0) | (z == replicas - 1)).astype(jnp.int32).reshape(1)
        up_far = turned_sum(up_kept[1], up_met[0][None], 0)
        gate_share = choose(outer, gate_far, gate_own, [up_far])
        down = grad_down(og_rows, [gate_share])
        up_far = outward(up_far, replicas, "up_sums")
        up_own = turned_sum(up_kept[0], up_met[1][None], 0, [down])
        token_grads, gate_grads = finish_tokens(sums, experts, tok_count, pick_width, [up_own])
        up_share = choose(outer, up_far, up_own, [token_grads])
    else:
        every = jnp.arange(replicas, dtype=jnp.int32)

        def scatter(grads):
            total = jnp.stack(weight_grad(x, grads, every, replicas))
            return lax.psum_scatter(total, "dp", scatter_dimension=0, tiled=True)[0].T[None]

        gate_share, up_share = scatter(gate_grad), scatter(up_grad)
        for t in range(1, replicas - 1):
            onward(t)
        sums = return_sums(input_grads(), experts, "token_grads")
        token_grads, gate_grads = finish_tokens(sums, experts, tok_count, pick_width)
        down = grad_down(gather_pairs(og_rows, experts, "out_grad_share"))
    return (
        token_grads,
        gate_grads,
        gate_share,
        up_share,
        down[None],
    )


def solution(mesh):
    rows = P(("groups", "expert", "dp"), None)
    weights = P("expert", None, None)
    return jax.shard_map(
        on_device,
        mesh=mesh,
        in_specs=(rows, rows, rows, rows, weights, weights, weights),
        out_specs=(
            rows,
            rows,
            P(("groups", "expert"), "dp", None),
            P(("groups", "expert"), "dp", None),
            P(("groups", "expert"), None, "dp"),
        ),
        check_vma=False,
    )
```

```python
import functools

import jax
import jax.numpy as jnp
from jax import lax
from jax.experimental import pallas as pl
from jax.experimental.pallas import tpu as pltpu
from jax.sharding import PartitionSpec as P

BF = jnp.bfloat16
F32 = jnp.float32
VMEM_SMALL = 28 * 1024 * 1024
VMEM_LARGE = 60 * 1024 * 1024
COST = pl.CostEstimate(flops=1000, bytes_accessed=1000, transcendentals=0)


def dot(a, b, ca, cb):
    return lax.dot_general(a, b, (((ca,), (cb,)), ((), ())), preferred_element_type=F32)


def send(x, axis, pairs, what):
    with jax.named_scope(what):
        return lax.ppermute(x, axis, pairs)


def core_swap(x, experts, what):
    return send(x, "expert", [(i, i ^ 1) for i in range(experts)], what + "_core")


def chip_shift(x, experts, k, what):
    return send(x, "expert", [((i + 2 * k) % experts, i) for i in range(experts)], what + "_chip")


def gather_pairs(x, experts, what):
    pairs = []
    for k in range(experts // 2):
        mine = x if k == 0 else chip_shift(x, experts, k, what)
        pairs.append((mine, core_swap(mine, experts, what)))
    return pairs


def flat(pairs):
    return [b for pair in pairs for b in pair]


def return_sums(pairs, experts, what):
    return [add(own, core_swap(other, experts, what)) for own, other in pairs]


def add(*terms):
    total = terms[0].astype(F32)
    for t in terms[1:]:
        total = total + t.astype(F32)
    return total.astype(terms[0].dtype)


def line_step(x, step, size, towards, what):
    if towards > 0:
        pairs = [(i, i + 1) for i in range(size - 1) if i >= step]
    else:
        pairs = [(i, i - 1) for i in range(1, size) if size - 1 - i >= step]
    return send(x, "dp", pairs, what + ("_right" if towards > 0 else "_left"))


def rotate(x, k, size, what):
    return send(x, "dp", [(i, (i + k) % size) for i in range(size)], what + "_rotated")


def inward(x, size, what):
    return send(x, "dp", [(0, 1), (size - 1, size - 2)], what + "_inward")


def outward(x, size, what):
    return send(x, "dp", [(1, 0), (size - 2, size - 1)], what + "_outward")


def across(x, what):
    return send(x, "dp", [(1, 2), (2, 1)], what + "_across")


def call(body, name, grid, inputs, outputs, scratch=(), deps=(), limit=VMEM_SMALL):
    def spec(entry):
        if len(entry) == 2:
            return pl.BlockSpec(memory_space=entry[1])
        return pl.BlockSpec(entry[1], entry[2])

    n = len(inputs)

    def kernel(*refs):
        body(*refs[:n], *refs[n + len(deps) :])

    return pl.pallas_call(
        kernel,
        grid=grid,
        in_specs=[spec(e) for e in inputs] + [pl.BlockSpec(memory_space=pl.ANY)] * len(deps),
        out_specs=[pl.BlockSpec(o[2], o[3]) for o in outputs],
        out_shape=[jax.ShapeDtypeStruct(o[0], o[1]) for o in outputs],
        scratch_shapes=list(scratch),
        compiler_params=pltpu.CompilerParams(vmem_limit_bytes=limit),
        cost_estimate=COST,
        name=name,
    )(*[e[0] for e in inputs], *deps)


def whole(a):
    return (a, a.shape, lambda *i: (0,) * a.ndim)


def copies(blocks, target, sem, first=0, axis=0):
    size = blocks[0].shape[axis]
    moves = []
    for i, b in enumerate(blocks):
        at = pl.ds(i * size, size)
        part = target.at[at] if axis == 0 else target.at[:, at]
        moves.append(pltpu.make_async_copy(b, part, sem.at[first + i]))
    return moves


def fetch(*args):
    moves = copies(*args)
    for m in moves:
        m.start()
    for m in moves:
        m.wait()


def turned(a, b):
    rows, cols = a.shape
    tile = 512

    def body(a, b, at, bt):
        at[...] = a[...].T
        bt[...] = b[...].T

    inputs = [(x, (tile, cols), lambda i: (i, 0)) for x in (a, b)]
    outputs = [((cols, rows), a.dtype, (cols, tile), lambda i: (0, i))] * 2
    return call(body, "turned", (rows // tile,), inputs, outputs)


def forward(pair, gate_wt, up_wt, deps=()):
    rows, width = 2 * pair[0].shape[0], pair[0].shape[1]
    units = gate_wt.shape[0]
    tile = 256

    def body(a, b, gate_wt, up_wt, hidden, gate_factor, up_factor, x, sem):
        @pl.when(pl.program_id(0) == 0)
        def _():
            fetch((a, b), x, sem)

        gate_pre = dot(gate_wt[...], x[...], 1, 1)
        up_pre = dot(up_wt[...], x[...], 1, 1)
        sigmoid = jax.nn.sigmoid(gate_pre)
        activated = gate_pre * sigmoid
        hidden[...] = (activated * up_pre).astype(BF)
        gate_factor[...] = (up_pre * (sigmoid * (1.0 + gate_pre * (1.0 - sigmoid)))).astype(BF)
        up_factor[...] = activated.astype(BF)

    at = lambda i: (i, 0)
    return call(
        body,
        "forward",
        (units // tile,),
        [(b, pltpu.HBM) for b in pair] + [(w, (tile, width), at) for w in (gate_wt, up_wt)],
        [((units, rows), t, (tile, rows), at) for t in (BF, BF, BF)],
        [pltpu.VMEM((rows, width), BF), pltpu.SemaphoreType.DMA((2,))],
        deps,
    )


def backward(pair, down_w, weight, hidden, gate_factor, up_factor, deps=()):
    rows, width = 2 * pair[0].shape[0], pair[0].shape[1]
    units = down_w.shape[0]
    tile = 256

    def body(
        a, b, down_w, weight, hidden, gate_factor, up_factor, gate_grad, up_grad, gate_sum, og, sem
    ):
        step = pl.program_id(0)

        @pl.when(step == 0)
        def _():
            fetch((a, b), og, sem)
            gate_sum[...] = jnp.zeros_like(gate_sum)

        raw = dot(down_w[...], og[...], 1, 1)
        scaled = raw * weight[...]
        gate_grad[...] = (scaled * gate_factor[...].astype(F32)).astype(BF)
        up_grad[...] = (scaled * up_factor[...].astype(F32)).astype(BF)
        gate_sum[...] += jnp.sum(raw * hidden[...].astype(F32), axis=0, keepdims=True)

    at = lambda i: (i, 0)
    tall = (tile, rows)
    return call(
        body,
        "backward",
        (units // tile,),
        [(b, pltpu.HBM) for b in pair]
        + [(down_w, (tile, width), at), whole(weight)]
        + [(a, tall, at) for a in (hidden, gate_factor, up_factor)],
        [((units, rows), BF, tall, at)] * 2 + [((1, rows), F32, (1, rows), lambda i: (0, 0))],
        [pltpu.VMEM((rows, width), BF), pltpu.SemaphoreType.DMA((2,))],
        deps,
    )


def slots(info, me, count):
    pairs, height, rows = info.shape
    width = height // 2

    def body(me, info, table, weight):
        chosen = info[0, :width] == me[0]
        weight[0] = jnp.sum(jnp.where(chosen, info[0, width:], 0.0), axis=0, keepdims=True)
        picked = jnp.sum(jnp.where(chosen, 1.0, 0.0), axis=0, keepdims=True)
        rank = jnp.broadcast_to(picked, (8, rows))
        lane = lax.broadcasted_iota(jnp.int32, (8, rows), 1)
        step = 1
        while step < rows:
            rank = rank + jnp.where(lane >= step, pltpu.roll(rank, step, 1), 0.0)
            step *= 2
        slot = jnp.where(picked > 0.0, rank[:1] - 1.0, float(count)).astype(jnp.int32)
        row = lax.broadcasted_iota(jnp.int32, (count, rows), 0)
        table[0] = jnp.where(row == slot, 1.0, 0.0).astype(BF)

    at = lambda i: (i, 0, 0)
    return call(
        body,
        "slots",
        (pairs,),
        [(me, pltpu.SMEM), (info, (1, height, rows), at)],
        [
            ((pairs, count, rows), BF, (1, count, rows), at),
            ((pairs, 1, rows), F32, (1, 1, rows), at),
        ],
    )


TAGS = 16


def pack(groups, tables, pairs, weight=None, deps=()):
    units, rows = groups[0][0].shape
    count = tables.shape[1]
    n = len(pairs)
    step = 256 if units % 256 == 0 else units
    inputs = [p for g in groups for p in g] + ([] if weight is None else [weight]) + [tables]

    def body(*refs):
        refs, outs = refs[: len(inputs)], refs[len(inputs) :]
        for i, c in enumerate(pairs):
            table = refs[-1][c]
            cols = slice(i * count, (i + 1) * count)
            for j in range(len(groups)):
                for start in range(0, units, step):
                    here = refs[j * n + i][start : start + step]
                    if weight is not None:
                        here = (here.astype(F32) * refs[-2][c]).astype(BF)
                    outs[j][start : start + step, cols] = dot(here, table, 1, 1).astype(BF)
            token = lax.broadcasted_iota(jnp.int32, (TAGS, rows), 1) + c * rows
            row = lax.broadcasted_iota(jnp.int32, (TAGS, rows), 0)
            token = jnp.where(row == 0, token // 256, jnp.where(row == 1, token % 256, 0))
            tags = dot(token.astype(F32).astype(BF), table, 1, 1)
            for out in outs:
                out[units:, cols] = tags.astype(BF)

    shape = (units + TAGS, n * count)
    return call(
        body,
        "pack",
        (1,),
        [whole(a) for a in inputs],
        [(shape, BF, shape, lambda i: (0, 0))] * len(groups),
        (),
        deps,
    )


def spread(packed, tags, rows, first=0):
    tags = tags.astype(F32)
    token = (tags[:1] * 256.0 + tags[1:2]).astype(jnp.int32) - first
    row = lax.broadcasted_iota(jnp.int32, (rows, packed.shape[1]), 0)
    table = jnp.where(row == token, 1.0, 0.0).astype(BF)
    return dot(packed, table, 1, 1).astype(BF)


def sum_products(packed, valid, blocks, order, parts, deps=()):
    height, width = blocks[0].shape
    rows, share = height * len(blocks), width // parts
    units = packed[0].shape[0] - TAGS
    m, n = len(packed), len(blocks)

    def body(valid, *refs):
        blocks, packed, (out, total, whole_rows, held, sem) = refs[:n], refs[n : n + m], refs[n + m :]
        moves = copies(blocks, whole_rows, sem)
        for move in moves:
            move.start()
        arrivals = [
            pltpu.make_async_copy(packed[i], held.at[i], sem.at[n + i]) for i in range(m)
        ]
        for move in arrivals:
            move.start()
        total[...] = jnp.zeros_like(total)
        for move in moves:
            move.wait()
        for i in range(m):
            arrivals[i].wait()

            @pl.when(valid[i] > 0)
            def _():
                left = spread(held[i, :units], held[i, units:], rows)
                cols = slice(order[i] * share, (order[i] + 1) * share)
                total[...] += dot(left, whole_rows[:, cols], 1, 0)

        out[...] = total[...].astype(BF)

    return call(
        body,
        "sum_products",
        (1,),
        [(valid, pltpu.SMEM)] + [(a, pltpu.HBM) for a in (*blocks, *packed)],
        [((units, share), BF, (units, share), lambda i: (0, 0))],
        [
            pltpu.VMEM((units, share), F32),
            pltpu.VMEM((rows, width), BF),
            pltpu.VMEM((m, *packed[0].shape), BF),
            pltpu.SemaphoreType.DMA((n + m,)),
        ],
        deps,
        VMEM_LARGE,
    )[0]


def input_grad(gate_grads, up_grads, gate_wt, up_wt, sums, deps=()):
    units, rows = gate_grads[0].shape
    width = gate_wt.shape[1]
    tile = 512
    half = rows // 2
    chips = len(gate_grads)
    picks = sums[0].shape[0]

    def body(*refs):
        grads, (gate_wt, up_wt), refs = refs[: 2 * chips], refs[2 * chips : 2 * chips + 2], refs[2 * chips + 2 :]
        sums, outs, turned = refs[:chips], refs[chips : 3 * chips], refs[3 * chips :]
        step = pl.program_id(0)

        @pl.when(step == 0)
        def _():
            for a, b in zip(grads, turned):
                b[...] = a[...].T

        for c in range(chips):
            total = dot(turned[c][...], gate_wt[...], 1, 0)
            total = total + dot(turned[chips + c][...], up_wt[...], 1, 0)
            for i in range(2):
                out = outs[2 * c + i]
                out[:half] = total[i * half : (i + 1) * half].astype(BF)
                out[half:] = jnp.zeros((TAGS, tile), BF)

                @pl.when(step == 0)
                def _():
                    left = sums[c][:, i * half : (i + 1) * half]
                    parts = []
                    for _ in range(3):
                        parts.append(left.astype(BF).astype(F32))
                        left = left - parts[-1]
                    parts.append(jnp.zeros((TAGS - 3 * picks, half), F32))
                    out[half:, :half] = jnp.concatenate(parts, axis=0).astype(BF)

    at = lambda i: (0, i)
    outs = call(
        body,
        "input_grad",
        (width // tile,),
        [whole(a) for a in (*gate_grads, *up_grads)]
        + [(w, (units, tile), at) for w in (gate_wt, up_wt)]
        + [whole(a) for a in sums],
        [((half + TAGS, width), BF, (half + TAGS, tile), at)] * (2 * chips),
        [pltpu.VMEM((rows, units), BF)] * (2 * chips),
        deps,
        VMEM_LARGE,
    )
    return [(outs[2 * c], outs[2 * c + 1]) for c in range(chips)]


def finish_tokens(sums, experts, tok_count, picks, deps=()):
    chips = experts // 2
    moved = [chip_shift(sums[k], experts, chips - k, "token_grads") for k in range(1, chips)]
    width = sums[0].shape[1]

    def body(*refs):
        refs, (grads, out) = refs[:chips], refs[chips:]
        total = refs[0][...].astype(F32)
        for ref in refs[1:]:
            total = total + ref[...].astype(F32)
        grads[...] = total[:tok_count].astype(BF)
        parts = total[tok_count:, :tok_count]
        out[...] = parts[:picks] + parts[picks : 2 * picks] + parts[2 * picks : 3 * picks]

    at = lambda i: (0, 0)
    grads, sums = call(
        body,
        "finish_tokens",
        (1,),
        [whole(a) for a in (sums[0], *moved)],
        [((tok_count, width), BF, (tok_count, width), at), ((picks, tok_count), F32, (picks, tok_count), at)],
        (),
        deps,
    )
    return grads, sums.T


def choose(flag, a, b, deps=()):
    def body(flag, a, b, out):
        out[0] = jnp.where(flag[0] > 0, a[...], b[...])

    return call(
        body,
        "choose",
        (1,),
        [(flag, pltpu.SMEM), whole(a), whole(b)],
        [((1, *a.shape), BF, (1, *a.shape), lambda i: (0, 0, 0))],
        (),
        deps,
    )[0]


def weight_grad(x_pairs, grads, shares, replicas, fold=None, deps=(), joined=False, space=pltpu.HBM):
    chips, n = len(x_pairs), shares.shape[0]
    blocks = flat(x_pairs)
    units, rows = grads[0].shape
    width = blocks[0].shape[1]
    packed = []
    if fold is not None:
        blocks = blocks + flat(fold[0])
        packed = [fold[1]]
    total = len(blocks) * blocks[0].shape[0]
    share = width // replicas

    own = len(x_pairs) * 2
    near = chips * rows

    def body(shares, *refs):
        blocks_in, refs = refs[: len(blocks)], refs[len(blocks) :]
        grads_in, refs = refs[:chips], refs[chips:]
        packed_in, refs = refs[: len(packed)], refs[len(packed) :]
        outs, (x, g, held, sem) = refs[:-4], refs[-4:]
        step = pl.program_id(0)
        cols = pl.ds(pl.multiple_of(shares[step] * share, share), share)

        def store(value):
            value = value.astype(BF)
            if joined:
                outs[0][0] = value
            else:
                for i, out in enumerate(outs):

                    @pl.when(step == i)
                    def _():
                        out[...] = value

        @pl.when(step == 0)
        def _():
            first = copies(grads_in, g, sem, 0, 1) + copies(blocks_in[:own], x, sem, chips)
            there = [
                pltpu.make_async_copy(p, held, sem.at[chips + len(blocks)]) for p in packed_in
            ]
            rest = []
            if fold is not None:
                rest = copies(blocks_in[own:], x.at[pl.ds(near, total - near)], sem, chips + own)
            for m in first + there + rest:
                m.start()
            for m in first:
                m.wait()
            value = dot(g[:, :near], x[:near, cols], 1, 0)
            for m in there:
                m.wait()
            if fold is not None:
                for i in range(chips):
                    part = slice(i * held.shape[1] // chips, (i + 1) * held.shape[1] // chips)
                    at = near + i * rows
                    g[:, at : at + rows] = spread(
                        held[:units, part], held[units:, part], rows, i * rows
                    )
            for m in rest:
                m.wait()
            if fold is not None:
                value = value + dot(g[:, near:], x[near:, cols], 1, 0)
            store(value)

        @pl.when(step > 0)
        def _():
            store(dot(g[...], x[:, cols], 1, 0))

    if joined:
        outputs = [((n, units, share), BF, (1, units, share), lambda i: (i, 0, 0))]
    else:
        outputs = [((units, share), BF, (units, share), lambda i: (0, 0))] * n
    return call(
        body,
        "weight_grad",
        (n,),
        [(shares, pltpu.SMEM)]
        + [(a, space) for a in (*blocks, *grads, *packed)],
        outputs,
        [
            pltpu.VMEM((total, width), BF),
            pltpu.VMEM((units, total), BF),
            pltpu.VMEM(packed[0].shape if packed else (16, 128), BF),
            pltpu.SemaphoreType.DMA((len(blocks) + chips + 1,)),
        ],
        deps,
        VMEM_LARGE,
    )


def turned_sum(a, b, part, deps=()):
    def body(a, b, out):
        out[...] = (a[...].astype(F32) + b[0].astype(F32)).T.astype(BF)

    shape = (a.shape[1], a.shape[0])
    return call(
        body,
        "turned_sum",
        (1,),
        [whole(a), (b, (1, *a.shape), lambda i: (part, 0, 0))],
        [(shape, BF, shape, lambda i: (0, 0))],
        (),
        deps,
    )[0]


def on_device(tokens, expert_ids, gate_weights, out_grad, w_gate, w_up, w_down):
    tok_count, pick_width = expert_ids.shape
    experts, replicas = lax.axis_size("expert"), lax.axis_size("dp")
    chips = experts // 2
    me, z = lax.axis_index("expert").astype(F32).reshape(1), lax.axis_index("dp")
    down_w = w_down[0]
    width = tokens.shape[1]
    share = width // replicas
    capacity = 4 * tok_count * pick_width // (3 * experts)
    count = experts * capacity
    pair_rows = 2 * tok_count
    folding = replicas == 4
    pairs = list(range(chips))
    meet = lax.optimization_barrier

    x_core = core_swap(tokens, experts, "tokens")
    x_fold = inward(tokens, replicas, "tokens") if folding else tokens
    x_far = [chip_shift(tokens, experts, k, "tokens") for k in range(1, chips)]
    info = jnp.concatenate([expert_ids.T.astype(F32), gate_weights.T], axis=0)
    info_far = [chip_shift(info, experts, k, "routing") for k in range(1, chips)]
    og_shares = []
    for k in range(replicas):
        part = lax.dynamic_slice_in_dim(out_grad, (z + k) % replicas * share, share, 1)
        og_shares.append(rotate(part, k, replicas, "out_grad_share") if k else part)
    gate_wt, up_wt = turned(w_gate[0], w_up[0])
    fwd = [forward((tokens, x_core), gate_wt, up_wt)]
    x_far, info, info_far, x_fold, out_grad, gate_wt, up_wt, fwd = meet(
        (x_far, info, info_far, x_fold, out_grad, gate_wt, up_wt, fwd)
    )

    og_core = core_swap(out_grad, experts, "out_grad")
    og_far = [chip_shift(out_grad, experts, k, "out_grad") for k in range(1, chips)]
    x = [(tokens, x_core)] + [(b, core_swap(b, experts, "tokens")) for b in x_far]
    info = [(b, core_swap(b, experts, "routing")) for b in (info, *info_far)]
    info = jnp.stack([jnp.concatenate(pair, axis=1) for pair in info])
    fwd += [forward(pair, gate_wt, up_wt) for pair in x[1:]]
    tables, weights = slots(info, me, count // chips)
    packed = pack([[f[0] for f in fwd]], tables, pairs, weights)[0]
    right = [line_step(packed, 0, replicas, 1, "hidden")]
    left = [line_step(packed, 0, replicas, -1, "hidden")]
    og_far, og_core, og_shares, packed, fwd, tables, weights, x, x_fold, info = meet(
        (og_far, og_core, og_shares, packed, fwd, tables, weights, x, x_fold, info)
    )

    def onward(t):
        right.append(line_step(right[-1], t, replicas, 1, "hidden"))
        left.append(line_step(left[-1], t, replicas, -1, "hidden"))

    bwd = [backward((out_grad, og_core), down_w, weights[0], *fwd[0])]
    for c in range(1, chips):
        pair = (og_far[c - 1], core_swap(og_far[c - 1], experts, "out_grad"))
        bwd.append(backward(pair, down_w, weights[c], *fwd[c]))
    gate_grad, up_grad = [b[0] for b in bwd], [b[1] for b in bwd]
    og_rows = jnp.concatenate(og_shares, axis=1)

    def input_grads(deps=()):
        sums = [jnp.where(info[c, :pick_width] == me, b[2], 0.0) for c, b in enumerate(bwd)]
        return input_grad([b[0] for b in bwd], [b[1] for b in bwd], gate_wt, up_wt, sums, deps)

    def grad_down(og_rows, deps=()):
        gathered, blocks, valid = [packed], [0], [z >= 0]
        for t in range(replicas - 1):
            gathered += [right[t], left[t]]
            blocks += [t + 1, replicas - 1 - t]
            valid += [z - 1 - t >= 0, z + 1 + t < replicas]
        valid = jnp.stack(valid).astype(jnp.int32)
        return sum_products(gathered, valid, flat(og_rows), blocks, replicas, deps)

    if folding:
        x_there = [chip_shift(x_fold, experts, k, "tokens_fold") for k in range(1, chips)]
        gate_packed, up_packed = pack([gate_grad, up_grad], tables, pairs)
        gate_there = inward(gate_packed, replicas, "gate_grad")
        up_there = inward(up_packed, replicas, "up_grad")
        right, left, bwd, gate_grad, up_grad, og_rows, x_there = meet(
            (right, left, bwd, gate_grad, up_grad, og_rows, x_there)
        )

        onward(1)
        x_there = [(b, core_swap(b, experts, "tokens_fold")) for b in [x_fold, *x_there]]
        og_rows = [og_rows, *(chip_shift(og_rows, experts, k, "out_grad_share") for k in range(1, chips))]
        gate_there, x_there, gate_grad = meet((gate_there, x_there, gate_grad))

        order = jnp.where(z < 2, jnp.arange(3, -1, -1), jnp.arange(4)).astype(jnp.int32)
        fold = (x_there, gate_there)
        gate_sent = weight_grad(x, gate_grad, order[:2], replicas, fold, (), True, pl.ANY)[0]
        gate_met = across(gate_sent, "gate_sums")
        og_rows = [(b, core_swap(b, experts, "out_grad_share")) for b in og_rows]
        up_there, gate_sent, gate_there, x_there, gate_grad, up_grad, right, left = meet(
            (up_there, gate_sent, gate_there, x_there, gate_grad, up_grad, right, left)
        )

        up_sent = weight_grad(x, up_grad, order[:2], replicas, (x_there, up_there))
        up_met = [across(up_sent[0], "up_far_sums"), across(up_sent[1], "up_sums")]
        gate_kept = weight_grad(x, gate_grad, order[2:], replicas, (x_there, gate_there), up_sent)
        onward(2)
        halves = input_grads(gate_kept)
        gate_met, gate_kept, up_grad, halves, og_rows, right, left = meet(
            (gate_met, gate_kept, up_grad, halves, og_rows, right, left)
        )
        up_kept = weight_grad(x, up_grad, order[2:], replicas, (x_there, up_there))

        gate_far = outward(turned_sum(gate_kept[1], gate_met, 0), replicas, "gate_sums")
        sums = return_sums(halves, experts, "token_grads")
        gate_own = turned_sum(gate_kept[0], gate_met, 1, up_kept)
        up_met[0], up_kept, gate_own = meet((up_met[0], up_kept, gate_own))

        outer = ((z == 0) | (z == replicas - 1)).astype(jnp.int32).reshape(1)
        up_far = turned_sum(up_kept[1], up_met[0][None], 0)
        gate_share = choose(outer, gate_far, gate_own, [up_far])
        down = grad_down(og_rows, [gate_share])
        up_far = outward(up_far, replicas, "up_sums")
        up_own = turned_sum(up_kept[0], up_met[1][None], 0, [down])
        token_grads, gate_grads = finish_tokens(sums, experts, tok_count, pick_width, [up_own])
        up_share = choose(outer, up_far, up_own, [token_grads])
    else:
        every = jnp.arange(replicas, dtype=jnp.int32)

        def scatter(grads):
            total = jnp.stack(weight_grad(x, grads, every, replicas))
            return lax.psum_scatter(total, "dp", scatter_dimension=0, tiled=True)[0].T[None]

        gate_share, up_share = scatter(gate_grad), scatter(up_grad)
        for t in range(1, replicas - 1):
            onward(t)
        sums = return_sums(input_grads(), experts, "token_grads")
        token_grads, gate_grads = finish_tokens(sums, experts, tok_count, pick_width)
        down = grad_down(gather_pairs(og_rows, experts, "out_grad_share"))
    return (
        token_grads,
        gate_grads,
        gate_share,
        up_share,
        down[None],
    )


def solution(mesh):
    rows = P(("groups", "expert", "dp"), None)
    weights = P("expert", None, None)
    return jax.shard_map(
        on_device,
        mesh=mesh,
        in_specs=(rows, rows, rows, rows, weights, weights, weights),
        out_specs=(
            rows,
            rows,
            P(("groups", "expert"), "dp", None),
            P(("groups", "expert"), "dp", None),
            P(("groups", "expert"), None, "dp"),
        ),
        check_vma=False,
    )
```
